32 devices in a mesh: view: 2 (over y), batch: 16 (over z, x, core).
Axes of the slice: x: 2, y: 2, z: 4, core: 2. Of those that a mesh axis runs over, the one named last changes fastest.
Arguments:
- embeddings: bfloat16 [2, 2048, 256], P('view', 'batch'), may hold values from -1.5 to 1.5
- positive: int32 [2, 2048], P(None, 'batch'), may hold values from 0 to 127, as said below
Outputs:
- gradients: float32 [2, 2048, 256], P('view', 'batch')
- totals: float32 [2, 2048], P('view', 'batch')
- row_loss: float32 [2, 2048], P('view', 'batch')
The draws below stay inside these ranges and needn't reach their ends.
Inputs may be any that keep to these rules, and one draw needn't show every extreme that they name: `positive`: for each view and each aligned block of 128 samples, the entries are a permutation of 0 to 127.
All inputs are finite; a program needn't handle non-finite values.
Results may differ from the reference program's by a relative error of at most 0.002.
Values may be sent and summed in bfloat16 or wider, within the bound.
A program may use at most 64 MiB of HBM per device.

```python
import jax
import jax.numpy as jnp
from jax import lax

ROWS = 128
EMBED = 256
VIEWS = 2
BATCH = 2048


def draw_embeddings(key, part):
    normal_key = jax.random.fold_in(key, 0)
    values = jnp.clip(jax.random.normal(normal_key, (VIEWS, BATCH, EMBED), jnp.float32) * 0.11, -1.5, 1.5)
    return values.astype(jnp.bfloat16)


def draw_positive(key, part):
    shard_count = VIEWS * (BATCH // ROWS)
    key_list = jax.random.split(key, shard_count)
    orders = jax.vmap(lambda sub_key: jax.random.permutation(sub_key, ROWS))(key_list)
    return orders.reshape(VIEWS, BATCH).astype(jnp.int32)


def setup_inputs(seed: int = 0) -> dict:
    seeds = jax.random.split(jax.random.key(seed), 3)
    return {
        "embeddings": draw_embeddings(jax.random.fold_in(seeds[2], 71), 0),
        "positive": draw_positive(jax.random.fold_in(seeds[2], 71), 0),
    }


logit_scale = 10.0


def pair_terms(anchor_emb, key_emb):
    block_count = BATCH // ROWS
    block_ids = jnp.arange(block_count, dtype=jnp.int32)

    def block_scores(block_id):
        anchor_rows = lax.dynamic_slice_in_dim(anchor_emb, (block_id * ROWS).astype(jnp.int32), ROWS, 0)
        scores = jnp.dot(anchor_rows, key_emb.T, preferred_element_type=jnp.float32) * logit_scale
        return anchor_rows, scores

    def first_pass(running, block_id):
        column_max, column_sum = running
        anchor_rows, scores = block_scores(block_id)
        row_max = jnp.max(scores, axis=1, keepdims=True)
        row_total = row_max[:, 0] + jnp.log(jnp.sum(jnp.exp(scores - row_max), axis=1))
        new_max = jnp.maximum(column_max, jnp.max(scores, axis=0))
        column_sum = column_sum * jnp.exp(column_max - new_max) + jnp.sum(jnp.exp(scores - new_max[None, :]), axis=0)
        return (new_max, column_sum), row_total

    start_state = (jnp.full((BATCH,), -1e30, jnp.float32), jnp.zeros((BATCH,), jnp.float32))
    (column_max, column_sum), row_blocks = lax.scan(first_pass, start_state, block_ids)
    anchor_totals = row_blocks.reshape(BATCH)
    key_totals = column_max + jnp.log(column_sum)

    def second_pass(running, block_id):
        key_own, key_side = running
        anchor_rows, scores = block_scores(block_id)
        row_totals = lax.dynamic_slice_in_dim(anchor_totals, (block_id * ROWS).astype(jnp.int32), ROWS, 0)
        w_rows = jnp.exp(scores - row_totals[:, None]).astype(jnp.bfloat16)
        w_cols = jnp.exp(scores - key_totals[None, :]).astype(jnp.bfloat16)
        anchor_own = jnp.dot(w_rows, key_emb, preferred_element_type=jnp.float32)
        anchor_side = jnp.dot(w_cols, key_emb, preferred_element_type=jnp.float32)
        key_own = key_own + jnp.dot(w_cols.T, anchor_rows, preferred_element_type=jnp.float32)
        key_side = key_side + jnp.dot(w_rows.T, anchor_rows, preferred_element_type=jnp.float32)
        return (key_own, key_side), (anchor_own, anchor_side)

    zero_acc = jnp.zeros((BATCH, EMBED), jnp.float32)
    (key_own, key_side), (anchor_own, anchor_side) = lax.scan(second_pass, (zero_acc, zero_acc), block_ids)
    anchor_own = anchor_own.reshape(BATCH, EMBED)
    anchor_side = anchor_side.reshape(BATCH, EMBED)
    return anchor_totals, anchor_own, anchor_side, key_totals, key_own, key_side


def reference(embeddings, positive):
    half_views = VIEWS // 2
    totals_list = [None] * VIEWS
    own_list = [None] * VIEWS
    side_list = [None] * VIEWS
    for anchor_view in range(half_views):
        key_view = anchor_view + half_views
        results = pair_terms(embeddings[anchor_view], embeddings[key_view])
        totals_list[anchor_view], own_list[anchor_view], side_list[anchor_view] = results[0], results[1], results[2]
        totals_list[key_view], own_list[key_view], side_list[key_view] = results[3], results[4], results[5]
    block_base = (jnp.arange(BATCH, dtype=jnp.int32) // ROWS) * ROWS
    grad_list = []
    loss_list = []
    for view_id in range(VIEWS):
        paired = (view_id + half_views) % VIEWS
        match_own = block_base + positive[view_id].astype(jnp.int32)
        match_far = block_base + positive[paired].astype(jnp.int32)
        pos_rows = embeddings[paired][match_own].astype(jnp.float32)
        pos_score = jnp.sum(embeddings[view_id].astype(jnp.float32) * pos_rows, axis=1) * logit_scale
        loss_list.append(totals_list[view_id] - pos_score)
        matched = jnp.zeros((BATCH, EMBED), jnp.float32).at[match_far].add(embeddings[paired].astype(jnp.float32))
        grad_list.append(logit_scale * (own_list[view_id] - pos_rows + side_list[view_id] - matched))
    return jnp.stack(grad_list), jnp.stack(totals_list), jnp.stack(loss_list)
```

```python
import functools
import math

import jax
import jax.numpy as jnp
from jax import lax
from jax.experimental import pallas as pl
from jax.experimental.pallas import tpu as pltpu
from jax.sharding import PartitionSpec as P

LOGIT_SCALE = 10.0
LOG2E = math.log2(math.e)
LN2 = math.log(2.0)
MESH = pl.DeviceIdType.MESH


def flip(value, mask):
    bit = 1
    while bit <= mask:
        if mask & bit:
            value = value + bit - 2 * bit * ((value // bit) % 2)
        bit *= 2
    return value


def kernel(views, devices, emb_ref, pos_ref, grad_ref, total_ref, loss_ref,
           own_ref, keys_ref, score_ref, total_send, total_all,
           own_sem, send_sem, direct_sem, cross_sem, core_sem, total_send_sem, total_sem):
    view = lax.axis_index("view")
    batch = lax.axis_index("batch")
    pair = lax.rem(view + views // 2, views)
    rows = own_ref.shape[0]
    lines = devices // 4

    sibling = flip(batch, 1)
    across = flip(batch, 2)

    def block(index):
        return keys_ref.at[pl.ds(pl.multiple_of(index * rows, rows), rows)]

    own_copy = pltpu.make_async_copy(emb_ref, own_ref, own_sem)
    own_copy.start()

    barrier = pltpu.get_barrier_semaphore()
    for step in range(devices):
        pl.semaphore_signal(barrier, inc=1, device_id=(pair, flip(batch, step)), device_id_type=MESH)
    pl.semaphore_signal(barrier, inc=1, device_id=(view, sibling), device_id_type=MESH)
    pl.semaphore_signal(barrier, inc=1, device_id=(view, across), device_id_type=MESH)
    pl.semaphore_wait(barrier, devices + 2)

    def direct(step):
        return pltpu.make_async_remote_copy(
            src_ref=emb_ref, dst_ref=block(batch), send_sem=send_sem, recv_sem=direct_sem.at[step],
            device_id=(pair, flip(batch, 4 * step)), device_id_type=MESH)

    def forward(index, target, sem):
        return pltpu.make_async_remote_copy(
            src_ref=block(index), dst_ref=block(index), send_sem=send_sem, recv_sem=sem,
            device_id=(view, target), device_id_type=MESH)

    for step in range(lines):
        direct(step).start()

    own_match = pos_ref[pl.ds(view, 1), :]
    far_match = pos_ref[pl.ds(pair, 1), :]
    lane_ids = lax.broadcasted_iota(jnp.int32, (rows, rows), 1)
    row_ids = lax.broadcasted_iota(jnp.int32, (rows, rows), 0)
    own_cols = jnp.broadcast_to(own_match.astype(jnp.float32), (rows, rows)).T
    own_hot = own_cols == lane_ids.astype(jnp.float32)
    far_hot = jnp.broadcast_to(far_match, (rows, rows)) == row_ids
    hot = (own_hot.astype(jnp.float32) + far_hot.astype(jnp.float32)).astype(jnp.bfloat16)
    own_copy.wait()

    def wait_on(index, sem):
        pltpu.make_async_remote_copy(
            src_ref=block(index), dst_ref=block(index), send_sem=send_sem, recv_sem=sem,
            device_id=(view, sibling), device_id_type=MESH).wait_recv()

    def take_direct(step):
        index = flip(batch, 4 * step)
        wait_on(index, direct_sem.at[step])
        forward(index, across, cross_sem.at[step]).start()
        forward(index, sibling, core_sem.at[2 * step]).start()

    def take_cross(step):
        index = flip(batch, 4 * step + 2)
        wait_on(index, cross_sem.at[step])
        forward(index, sibling, core_sem.at[2 * step + 1]).start()

    order = []

    def chunk_base(slot):
        step, side = slot // 2, slot % 2
        chip = flip(batch // 2, 2 * step + side)
        return chip

    def chunk(slot):
        return pl.ds(pl.multiple_of(chunk_base(slot) * (2 * rows), 2 * rows), 2 * rows)

    top = None

    def take_core(slot, top):
        step, side = slot // 2, slot % 2
        wait_on(flip(batch, 4 * step + 2 * side + 1), core_sem.at[slot])
        scores = lax.dot_general(own_ref[...], keys_ref[chunk(slot), :], (((1,), (1,)), ((), ())),
                                 preferred_element_type=jnp.float32) * (LOGIT_SCALE * LOG2E)
        score_ref[slot] = scores
        order.append(slot)
        return scores if top is None else jnp.maximum(top, scores)

    take_direct(0)
    for step in range(1, lines + 1):
        if step < lines:
            take_direct(step)
        take_cross(step - 1)
        top = take_core(2 * (step - 1), top)
        if step >= 2:
            top = take_core(2 * (step - 2) + 1, top)
        if step == 1:
            base = jnp.dot(hot, block(batch)[...], preferred_element_type=jnp.float32)
    top = take_core(2 * (lines - 1) + 1, top)

    row_max = jnp.max(top, axis=1, keepdims=True)
    summed = jnp.zeros((rows, 2 * rows), jnp.float32)
    for slot in order:
        summed = summed + jnp.exp2(score_ref[slot] - row_max)
    row_total = row_max + jnp.log(jnp.sum(summed, axis=1, keepdims=True)) * LOG2E

    first = score_ref[0]
    own_score = jnp.where(lax.rem(batch, 2) == 0, first[:, :rows], first[:, rows:])
    pos_score = jnp.sum(jnp.where(own_hot, own_score, 0.0), axis=1, keepdims=True)
    packed = jnp.where(lane_ids == 0, row_total, row_total - pos_score).T
    total_send[...] = packed[0:1, :]

    def send_total(step):
        return pltpu.make_async_remote_copy(
            src_ref=total_send, dst_ref=total_all.at[batch], send_sem=total_send_sem, recv_sem=total_sem,
            device_id=(pair, flip(batch, step)), device_id_type=MESH)

    for step in range(devices):
        send_total(step).start()
    total_ref[...] = packed[0:1, :] * LN2
    loss_ref[...] = packed[1:2, :] * LN2

    spread = -base
    for slot in order:
        weights = jnp.exp2(score_ref[slot] - row_total).astype(jnp.bfloat16)
        spread = spread + jnp.dot(weights, keys_ref[chunk(slot), :], preferred_element_type=jnp.float32)

    pltpu.make_async_remote_copy(
        src_ref=total_all, dst_ref=total_all, send_sem=total_send_sem, recv_sem=total_sem,
        device_id=(view, sibling), device_id_type=MESH).wait()
    for slot in order:
        chip = chunk_base(slot)
        far_total = jnp.concatenate([total_all[2 * chip], total_all[2 * chip + 1]], axis=1)
        weights = jnp.exp2(score_ref[slot] - far_total).astype(jnp.bfloat16)
        spread = spread + jnp.dot(weights, keys_ref[chunk(slot), :], preferred_element_type=jnp.float32)
    grad_ref[...] = spread * LOGIT_SCALE
    pltpu.make_async_remote_copy(
        src_ref=keys_ref, dst_ref=keys_ref, send_sem=send_sem, recv_sem=total_sem,
        device_id=(view, sibling), device_id_type=MESH).wait_send()


def body(views, devices, embeddings, positive):
    _, rows, width = embeddings.shape
    lines = devices // 4
    slots = devices // 2
    vmem = pl.BlockSpec(memory_space=pltpu.VMEM)
    grads, totals, losses = pl.pallas_call(
        functools.partial(kernel, views, devices),
        out_shape=(
            jax.ShapeDtypeStruct((rows, width), jnp.float32),
            jax.ShapeDtypeStruct((1, rows), jnp.float32),
            jax.ShapeDtypeStruct((1, rows), jnp.float32),
        ),
        in_specs=[pl.BlockSpec(memory_space=pl.ANY), vmem],
        out_specs=(vmem, vmem, vmem),
        scratch_shapes=[
            pltpu.VMEM((rows, width), jnp.bfloat16),
            pltpu.VMEM((devices * rows, width), jnp.bfloat16),
            pltpu.VMEM((slots, rows, 2 * rows), jnp.float32),
            pltpu.VMEM((1, rows), jnp.float32),
            pltpu.VMEM((devices, 1, rows), jnp.float32),
            pltpu.SemaphoreType.DMA,
            pltpu.SemaphoreType.DMA,
            pltpu.SemaphoreType.DMA((lines,)),
            pltpu.SemaphoreType.DMA((lines,)),
            pltpu.SemaphoreType.DMA((slots,)),
            pltpu.SemaphoreType.DMA,
            pltpu.SemaphoreType.DMA,
        ],
        compiler_params=pltpu.CompilerParams(
            collective_id=0, has_side_effects=True, vmem_limit_bytes=32 * 1024 * 1024),
    )(embeddings.reshape(rows, width), positive)
    return grads[None], totals, losses


def solution(mesh):
    return jax.shard_map(
        functools.partial(body, mesh.shape["view"], mesh.shape["batch"]),
        mesh=mesh,
        in_specs=(P("view", "batch", None), P(None, "batch")),
        out_specs=(P("view", "batch", None), P("view", "batch"), P("view", "batch")),
        check_vma=False,
    )
```

```python
import functools
import math

import jax
import jax.numpy as jnp
from jax import lax
from jax.experimental import pallas as pl
from jax.experimental.pallas import tpu as pltpu
from jax.sharding import PartitionSpec as P

LOGIT_SCALE = 10.0
LOG2E = math.log2(math.e)
LN2 = math.log(2.0)
MESH = pl.DeviceIdType.MESH


def flip(value, mask):
    bit = 1
    while bit <= mask:
        if mask & bit:
            value = value + bit - 2 * bit * ((value // bit) % 2)
        bit *= 2
    return value


def merge(first, second):
    top = jnp.maximum(first, second)
    return top + jnp.log(jnp.exp2(first - top) + jnp.exp2(second - top)) * LOG2E


def kernel(views, devices, emb_ref, pos_hbm, grad_ref, total_ref, loss_ref,
           own_ref, pos_ref, keys_ref, score_ref, weight_ref, part_send, part_near, part_far, grad_send, grad_near,
           local_sem, send_sem, near_send_sem, near_sem, direct_sem, core_sem, far_send_sem, far_sem):
    view = lax.axis_index("view")
    batch = lax.axis_index("batch")
    pair = lax.rem(view + views // 2, views)
    rows = own_ref.shape[0] // 2
    lines = devices // 4
    line = batch // 4
    core = lax.rem(batch, 2)
    sibling = flip(batch, 1)
    across = flip(batch, 2)

    own_copy = pltpu.make_async_copy(emb_ref, own_ref.at[pl.ds(0, rows)], local_sem.at[0])
    own_copy.start()
    pos_copy = pltpu.make_async_copy(pos_hbm, pos_ref, local_sem.at[1])
    pos_copy.start()

    barrier = pltpu.get_barrier_semaphore()
    for step in reversed(range(devices)):
        pl.semaphore_signal(barrier, inc=1, device_id=(pair, flip(batch, step)), device_id_type=MESH)
    pl.semaphore_signal(barrier, inc=1, device_id=(view, across), device_id_type=MESH)
    pl.semaphore_signal(barrier, inc=1, device_id=(view, sibling), device_id_type=MESH)

    own_copy.wait()
    pos_copy.wait()
    own_match = pos_ref[pl.ds(view, 1), :]
    far_match = pos_ref[pl.ds(pair, 1), :]
    lane_ids = lax.broadcasted_iota(jnp.int32, (rows, rows), 1)
    row_ids = lax.broadcasted_iota(jnp.int32, (rows, rows), 0)
    own_cols = jnp.broadcast_to(own_match.astype(jnp.float32), (rows, rows)).T
    own_hot = own_cols == lane_ids.astype(jnp.float32)
    far_hot = jnp.broadcast_to(far_match, (rows, rows)) == row_ids
    hot = (own_hot.astype(jnp.float32) + far_hot.astype(jnp.float32)).astype(jnp.bfloat16)

    pl.semaphore_wait(barrier, devices + 2)

    def block(chain, side):
        return keys_ref.at[pl.ds(pl.multiple_of((2 * chain + side) * rows, rows), rows)]

    def near(src, dst, index):
        return pltpu.make_async_remote_copy(
            src_ref=src, dst_ref=dst, send_sem=near_send_sem.at[index], recv_sem=near_sem.at[index],
            device_id=(view, across), device_id_type=MESH)

    def direct(step):
        return pltpu.make_async_remote_copy(
            src_ref=emb_ref, dst_ref=block(line, core), send_sem=send_sem, recv_sem=direct_sem.at[step],
            device_id=(pair, flip(batch, 4 * step)), device_id_type=MESH)

    def to_sibling(chain, side, sem):
        return pltpu.make_async_remote_copy(
            src_ref=block(chain, side), dst_ref=block(chain, side), send_sem=send_sem, recv_sem=sem,
            device_id=(view, sibling), device_id_type=MESH)

    anchors_copy = near(emb_ref, own_ref.at[pl.ds(rows, rows)], 0)
    for step in range(lines):
        direct(step).start()
    anchors_copy.start()

    def take_direct(step):
        chain = flip(line, step)
        to_sibling(chain, core, direct_sem.at[step]).wait_recv()
        to_sibling(chain, core, core_sem.at[step]).start()

    def chunk(step):
        return keys_ref[pl.ds(pl.multiple_of(flip(line, step) * (2 * rows), 2 * rows), 2 * rows), :]

    def take_core(step, top):
        to_sibling(flip(line, step), 1 - core, core_sem.at[step]).wait_recv()
        scores = lax.dot_general(own_ref[...], chunk(step), (((1,), (1,)), ((), ())),
                                 preferred_element_type=jnp.float32) * (LOGIT_SCALE * LOG2E)
        score_ref[step] = scores
        return scores if top is None else jnp.maximum(top, scores)

    top = None
    for step in range(lines):
        take_direct(step)
        if step == 0:
            base = jnp.dot(hot, block(line, core)[...], preferred_element_type=jnp.float32)
            anchors_copy.wait_recv()
        if step >= 1:
            top = take_core(step - 1, top)
    top = take_core(lines - 1, top)

    row_max = jnp.max(top, axis=1, keepdims=True)
    summed = jnp.zeros((2 * rows, 2 * rows), jnp.float32)
    for step in range(lines):
        summed = summed + jnp.exp2(score_ref[step] - row_max)
    row_part = row_max + jnp.log(jnp.sum(summed, axis=1, keepdims=True)) * LOG2E

    first = score_ref[0, :rows, :]
    own_score = jnp.where(core == 0, first[:, :rows], first[:, rows:])
    pos_score = jnp.sum(jnp.where(own_hot, own_score, 0.0), axis=1, keepdims=True)
    packed = jnp.where(lane_ids == 0, row_part[:rows], jnp.where(lane_ids == 1, row_part[rows:], pos_score)).T
    part_send[0] = packed[0:1, :]
    part_send[1] = packed[1:2, :]

    near_copy = near(part_send, part_near, 1)
    near_copy.start()
    for step in reversed(range(devices)):
        pltpu.make_async_remote_copy(
            src_ref=part_send.at[(step // 2) % 2], dst_ref=part_far.at[batch],
            send_sem=far_send_sem, recv_sem=far_sem,
            device_id=(pair, flip(batch, step)), device_id_type=MESH).start()

    near_copy.wait_recv()
    own_total = merge(packed[0:1, :], part_near[1])
    across_total = merge(packed[1:2, :], part_near[0])
    total_ref[...] = own_total * LN2
    loss_ref[...] = (own_total - packed[2:3, :]) * LN2

    def column(values):
        tall = jnp.broadcast_to(values, (rows, rows)).T
        return jnp.concatenate([tall, tall], axis=1)

    for half, values in enumerate((own_total, across_total)):
        tall = column(values)
        for step in range(lines):
            weight_ref[step, half * rows:(half + 1) * rows, :] = jnp.exp2(
                score_ref[step, half * rows:(half + 1) * rows, :] - tall)

    pltpu.make_async_remote_copy(
        src_ref=part_far, dst_ref=part_far, send_sem=far_send_sem, recv_sem=far_sem,
        device_id=(view, sibling), device_id_type=MESH).wait()

    def far_total(step):
        start = 4 * flip(line, step)
        return jnp.concatenate(
            [merge(part_far[start + side], part_far[start + 2 + side]) for side in range(2)], axis=1)

    far_totals = [far_total(step) for step in range(lines)]

    def spread(half, result):
        for step in range(lines):
            span = slice(half * rows, (half + 1) * rows)
            weights = weight_ref[step, span, :] + jnp.exp2(score_ref[step, span, :] - far_totals[step])
            part = jnp.dot(weights.astype(jnp.bfloat16), chunk(step), preferred_element_type=jnp.float32)
            result = part if result is None else result + part
        return result

    grad_send[...] = spread(1, None)
    grad_copy = near(grad_send, grad_near, 2)
    grad_copy.start()
    own_spread = spread(0, -base)
    anchors_copy.wait_send()
    near_copy.wait_send()
    pltpu.make_async_remote_copy(
        src_ref=keys_ref, dst_ref=keys_ref, send_sem=send_sem, recv_sem=far_sem,
        device_id=(view, sibling), device_id_type=MESH).wait_send()
    grad_copy.wait_recv()
    grad_ref[...] = (own_spread + grad_near[...]) * LOGIT_SCALE
    grad_copy.wait_send()


def body(views, devices, embeddings, positive):
    _, rows, width = embeddings.shape
    lines = devices // 4
    vmem = pl.BlockSpec(memory_space=pltpu.VMEM)
    hbm = pl.BlockSpec(memory_space=pltpu.HBM)
    dma = pltpu.SemaphoreType.DMA
    grads, totals, losses = pl.pallas_call(
        functools.partial(kernel, views, devices),
        out_shape=(
            jax.ShapeDtypeStruct((rows, width), jnp.float32),
            jax.ShapeDtypeStruct((1, rows), jnp.float32),
            jax.ShapeDtypeStruct((1, rows), jnp.float32),
        ),
        in_specs=[hbm, hbm],
        out_specs=(vmem, vmem, vmem),
        scratch_shapes=[
            pltpu.VMEM((2 * rows, width), jnp.bfloat16),
            pltpu.VMEM(positive.shape, jnp.int32),
            pltpu.VMEM((2 * lines * rows, width), jnp.bfloat16),
            pltpu.VMEM((lines, 2 * rows, 2 * rows), jnp.float32),
            pltpu.VMEM((lines, 2 * rows, 2 * rows), jnp.float32),
            pltpu.VMEM((2, 1, rows), jnp.float32),
            pltpu.VMEM((2, 1, rows), jnp.float32),
            pltpu.VMEM((devices, 1, rows), jnp.float32),
            pltpu.VMEM((rows, width), jnp.float32),
            pltpu.VMEM((rows, width), jnp.float32),
            dma((2,)), dma, dma((3,)), dma((3,)), dma((lines,)), dma((lines,)), dma, dma,
        ],
        compiler_params=pltpu.CompilerParams(
            collective_id=0, has_side_effects=True, vmem_limit_bytes=60 * 1024 * 1024),
    )(embeddings.reshape(rows, width), positive)
    return grads[None], totals, losses


def solution(mesh):
    return jax.shard_map(
        functools.partial(body, mesh.shape["view"], mesh.shape["batch"]),
        mesh=mesh,
        in_specs=(P("view", "batch", None), P(None, "batch")),
        out_specs=(P("view", "batch", None), P("view", "batch"), P("view", "batch")),
        check_vma=False,
    )
```

```python
import functools
import math

import jax
import jax.numpy as jnp
from jax import lax
from jax.experimental import pallas as pl
from jax.experimental.pallas import tpu as pltpu
from jax.sharding import PartitionSpec as P

LOGIT_SCALE = 10.0
LOG2E = math.log2(math.e)
LN2 = math.log(2.0)
MESH = pl.DeviceIdType.MESH


def flip(value, mask):
    bit = 1
    while bit <= mask:
        if mask & bit:
            value = value + bit - 2 * bit * ((value // bit) % 2)
        bit *= 2
    return value


def merge(first, second):
    top = jnp.maximum(first, second)
    return top + jnp.log(jnp.exp2(first - top) + jnp.exp2(second - top)) * LOG2E


def kernel(views, devices, emb_ref, pos_hbm, grad_ref, stats_ref,
           own_ref, pos_ref, keys_ref, score_ref, weight_ref, part_send, part_near, part_far, grad_send, grad_near,
           local_sem, send_sem, near_send_sem, near_sem, direct_sem, core_sem, far_send_sem, far_sem):
    view = lax.axis_index("view")
    batch = lax.axis_index("batch")
    pair = lax.rem(view + views // 2, views)
    rows = own_ref.shape[0] // 2
    lines = devices // 4
    line = batch // 4
    core = lax.rem(batch, 2)
    sibling = flip(batch, 1)
    across = flip(batch, 2)

    own_copy = pltpu.make_async_copy(emb_ref, own_ref.at[pl.ds(0, rows)], local_sem.at[0])
    own_copy.start()
    pos_copy = pltpu.make_async_copy(pos_hbm, pos_ref, local_sem.at[1])
    pos_copy.start()

    barrier = pltpu.get_barrier_semaphore()
    for step in reversed(range(devices)):
        pl.semaphore_signal(barrier, inc=1, device_id=(pair, flip(batch, step)), device_id_type=MESH)
    pl.semaphore_signal(barrier, inc=1, device_id=(view, across), device_id_type=MESH)
    pl.semaphore_signal(barrier, inc=1, device_id=(view, sibling), device_id_type=MESH)

    own_copy.wait()
    pos_copy.wait()
    own_match = pos_ref[pl.ds(view, 1), :]
    far_match = pos_ref[pl.ds(pair, 1), :]
    lane_ids = lax.broadcasted_iota(jnp.int32, (rows, rows), 1)
    row_ids = lax.broadcasted_iota(jnp.int32, (rows, rows), 0)
    own_cols = jnp.broadcast_to(own_match.astype(jnp.float32), (rows, rows)).T
    own_hot = own_cols == lane_ids.astype(jnp.float32)
    far_hot = jnp.broadcast_to(far_match, (rows, rows)) == row_ids
    hot = (own_hot.astype(jnp.float32) + far_hot.astype(jnp.float32)).astype(jnp.bfloat16)

    pl.semaphore_wait(barrier, devices + 2)

    def block(chain, side):
        return keys_ref.at[pl.ds(pl.multiple_of((2 * chain + side) * rows, rows), rows)]

    def near(src, dst, index):
        return pltpu.make_async_remote_copy(
            src_ref=src, dst_ref=dst, send_sem=near_send_sem.at[index], recv_sem=near_sem.at[index],
            device_id=(view, across), device_id_type=MESH)

    def direct(step):
        return pltpu.make_async_remote_copy(
            src_ref=emb_ref, dst_ref=block(line, core), send_sem=send_sem, recv_sem=direct_sem.at[step],
            device_id=(pair, flip(batch, 4 * step)), device_id_type=MESH)

    def to_sibling(chain, side, sem):
        return pltpu.make_async_remote_copy(
            src_ref=block(chain, side), dst_ref=block(chain, side), send_sem=send_sem, recv_sem=sem,
            device_id=(view, sibling), device_id_type=MESH)

    anchors_copy = near(emb_ref, own_ref.at[pl.ds(rows, rows)], 0)
    for step in range(lines):
        direct(step).start()
    anchors_copy.start()

    def take_direct(step):
        chain = flip(line, step)
        to_sibling(chain, core, direct_sem.at[step]).wait_recv()
        to_sibling(chain, core, core_sem.at[step]).start()

    def chunk(step):
        return keys_ref[pl.ds(pl.multiple_of(flip(line, step) * (2 * rows), 2 * rows), 2 * rows), :]

    def take_core(step, top):
        to_sibling(flip(line, step), 1 - core, core_sem.at[step]).wait_recv()
        scores = lax.dot_general(own_ref[...], chunk(step), (((1,), (1,)), ((), ())),
                                 preferred_element_type=jnp.float32) * (LOGIT_SCALE * LOG2E)
        score_ref[step] = scores
        return scores if top is None else jnp.maximum(top, scores)

    top = None
    for step in range(lines):
        take_direct(step)
        if step == 0:
            base = jnp.dot(hot, block(line, core)[...], preferred_element_type=jnp.float32)
            anchors_copy.wait_recv()
        if step >= 1:
            top = take_core(step - 1, top)
    top = take_core(lines - 1, top)

    row_max = jnp.max(top, axis=1, keepdims=True)
    summed = jnp.zeros((2 * rows, 2 * rows), jnp.float32)
    for step in range(lines):
        summed = summed + jnp.exp2(score_ref[step] - row_max)
    row_part = row_max + jnp.log(jnp.sum(summed, axis=1, keepdims=True)) * LOG2E

    first = score_ref[0, :rows, :]
    own_score = jnp.where(core == 0, first[:, :rows], first[:, rows:])
    pos_score = jnp.sum(jnp.where(own_hot, own_score, 0.0), axis=1, keepdims=True)
    packed = jnp.where(lane_ids == 0, row_part[:rows], jnp.where(lane_ids == 1, row_part[rows:], pos_score)).T
    part_send[0] = packed[0:1, :]
    part_send[1] = packed[1:2, :]

    near_copy = near(part_send, part_near, 1)
    near_copy.start()
    for step in reversed(range(devices)):
        pltpu.make_async_remote_copy(
            src_ref=part_send.at[(step // 2) % 2], dst_ref=part_far.at[batch],
            send_sem=far_send_sem, recv_sem=far_sem,
            device_id=(pair, flip(batch, step)), device_id_type=MESH).start()

    near_copy.wait_recv()
    own_total = merge(packed[0:1, :], part_near[1])
    across_total = merge(packed[1:2, :], part_near[0])
    stats_ref[0:1, :] = own_total
    stats_ref[1:2, :] = own_total - packed[2:3, :]

    def column(values):
        tall = jnp.broadcast_to(values, (rows, rows)).T
        return jnp.concatenate([tall, tall], axis=1)

    for half, values in enumerate((own_total, across_total)):
        tall = column(values)
        for step in range(lines):
            weight_ref[step, half * rows:(half + 1) * rows, :] = jnp.exp2(
                score_ref[step, half * rows:(half + 1) * rows, :] - tall)

    pltpu.make_async_remote_copy(
        src_ref=part_far, dst_ref=part_far, send_sem=far_send_sem, recv_sem=far_sem,
        device_id=(view, sibling), device_id_type=MESH).wait()

    def far_total(step):
        start = 4 * flip(line, step)
        return jnp.concatenate(
            [merge(part_far[start + side], part_far[start + 2 + side]) for side in range(2)], axis=1)

    far_totals = [far_total(step) for step in range(lines)]

    def spread(half, result):
        for step in range(lines):
            span = slice(half * rows, (half + 1) * rows)
            weights = weight_ref[step, span, :] + jnp.exp2(score_ref[step, span, :] - far_totals[step])
            part = jnp.dot(weights.astype(jnp.bfloat16), chunk(step), preferred_element_type=jnp.float32)
            result = part if result is None else result + part
        return result

    grad_send[...] = spread(1, None).astype(grad_send.dtype)
    grad_copy = near(grad_send, grad_near, 2)
    grad_copy.start()
    own_spread = spread(0, -base)
    anchors_copy.wait_send()
    near_copy.wait_send()
    pltpu.make_async_remote_copy(
        src_ref=keys_ref, dst_ref=keys_ref, send_sem=send_sem, recv_sem=far_sem,
        device_id=(view, sibling), device_id_type=MESH).wait_send()
    grad_copy.wait_recv()
    grad_ref[...] = own_spread + grad_near[...].astype(jnp.float32)
    grad_copy.wait_send()


def finish(spread_ref, stats_ref, grad_ref, total_ref, loss_ref):
    grad_ref[...] = spread_ref[...] * LOGIT_SCALE
    total_ref[...] = stats_ref[0:1, :] * LN2
    loss_ref[...] = stats_ref[1:2, :] * LN2


def body(views, devices, embeddings, positive):
    _, rows, width = embeddings.shape
    lines = devices // 4
    vmem = pl.BlockSpec(memory_space=pltpu.VMEM)
    hbm = pl.BlockSpec(memory_space=pltpu.HBM)
    dma = pltpu.SemaphoreType.DMA
    spread, stats = pl.pallas_call(
        functools.partial(kernel, views, devices),
        out_shape=(
            jax.ShapeDtypeStruct((rows, width), jnp.float32),
            jax.ShapeDtypeStruct((2, rows), jnp.float32),
        ),
        in_specs=[hbm, hbm],
        out_specs=(vmem, vmem),
        scratch_shapes=[
            pltpu.VMEM((2 * rows, width), jnp.bfloat16),
            pltpu.VMEM(positive.shape, jnp.int32),
            pltpu.VMEM((2 * lines * rows, width), jnp.bfloat16),
            pltpu.VMEM((lines, 2 * rows, 2 * rows), jnp.float32),
            pltpu.VMEM((lines, 2 * rows, 2 * rows), jnp.float32),
            pltpu.VMEM((2, 1, rows), jnp.float32),
            pltpu.VMEM((2, 1, rows), jnp.float32),
            pltpu.VMEM((devices, 1, rows), jnp.float32),
            pltpu.VMEM((rows, width), jnp.bfloat16),
            pltpu.VMEM((rows, width), jnp.bfloat16),
            dma((2,)), dma, dma((3,)), dma((3,)), dma((lines,)), dma((lines,)), dma, dma,
        ],
        compiler_params=pltpu.CompilerParams(
            collective_id=0, has_side_effects=True, vmem_limit_bytes=60 * 1024 * 1024),
    )(embeddings.reshape(rows, width), positive)
    grads, totals, losses = pl.pallas_call(
        finish,
        out_shape=(
            jax.ShapeDtypeStruct((rows, width), jnp.float32),
            jax.ShapeDtypeStruct((1, rows), jnp.float32),
            jax.ShapeDtypeStruct((1, rows), jnp.float32),
        ),
        in_specs=[vmem, vmem],
        out_specs=(vmem, vmem, vmem),
    )(spread, stats)
    return grads[None], totals, losses


def solution(mesh):
    return jax.shard_map(
        functools.partial(body, mesh.shape["view"], mesh.shape["batch"]),
        mesh=mesh,
        in_specs=(P("view", "batch", None), P(None, "batch")),
        out_specs=(P("view", "batch", None), P("view", "batch"), P("view", "batch")),
        check_vma=False,
    )
```
